128 devices in a mesh: seq: 4 (over z), chan: 32 (over x, y, core).
Axes of the slice: x: 4, y: 4, z: 4, core: 2. Of those that a mesh axis runs over, the one named last changes fastest.
Arguments:
- query_rows: bfloat16 [16384, 4096], P(('seq', 'chan')), may hold values from -6 to 6
- key_rows: bfloat16 [16384, 4096], P(('seq', 'chan')), may hold values from -6 to 6
- value_rows: bfloat16 [16384, 4096], P(('seq', 'chan')), may hold values from -6 to 6
- residue: float32 [4096, 16], P('chan'), may hold values from -1.5 to 1.5
- pole_rate: float32 [4096, 16], P('chan'), may hold values from 1 to 512
- skip_gain: float32 [4096], P('chan'), may hold values from -4 to 4
- out_weight: bfloat16 [4096, 4096], P('chan', 'seq'), may hold values from -0.09375 to 0.09375
Outputs:
- projected: bfloat16 [4, 4096, 4096], P(None, 'chan', 'seq')
The draws below stay inside these ranges and needn't reach their ends.
All inputs are finite; a program needn't handle non-finite values.
Results may differ from the reference program's by a relative error of at most 0.014.
Values may be sent and summed in bfloat16 or wider, within the bound.
No kernel may reach another device: no remote copies, remote signals or barrier semaphores. Data moves between devices by JAX's collectives and lax.ppermute only.
A program may use at most 192 MiB of HBM per device.

```python
import math
import jax
import jax.numpy as jnp
from jax import lax

D = 4096
ORDER = 16
TOK_SEQ = 4096
L = 16384
N_SEQ = 4


def levels(key, dims, shards, smallest, high):
    gain, own = 1.0, jax.random.fold_in(key, 6)
    for axis_at, shards_of in shards:
        draws = jnp.exp(jax.random.uniform(jax.random.fold_in(own, axis_at), (shards_of,), jnp.float32, smallest / len(shards), high / len(shards)))
        gain = gain * jnp.repeat(draws, dims[axis_at] // shards_of).reshape([-1 if axis == axis_at else 1 for axis in range(len(dims))])
    return gain


def scatter_about(stream_key, shape, spread, bound, pieces=(), held_as=jnp.bfloat16):
    result = spread * jax.random.normal(stream_key, shape, jnp.float32)
    if pieces:
        result = result * levels(stream_key, shape, pieces, -0.22, 0.18)
    return jnp.clip(result, -bound, bound).astype(held_as)


def setup_inputs(seed: int = 0) -> dict:
    key_list = jax.random.split(jax.random.key(seed), 8)
    query_rows = scatter_about(key_list[0], (L, D), 1.0, 6.0, ((0, 128),))
    key_rows = scatter_about(key_list[1], (L, D), 1.0, 6.0, ((0, 128),))
    value_rows = scatter_about(key_list[2], (L, D), 1.0, 6.0, ((0, 128),))
    residue = scatter_about(key_list[3], (D, ORDER), 0.25, 1.5, ((0, 32),), jnp.float32)
    pole_rate = jnp.clip(jnp.exp(math.log(512.0) - 6.2383246 * jax.random.uniform(key_list[4], (D, ORDER), jnp.float32) ** levels(key_list[4], (D, ORDER), ((0, 32),), -0.2, 0.2)), 1.0, 512.0)
    skip_gain = scatter_about(key_list[5], (D,), 1.0, 4.0, ((0, 32),), jnp.float32)
    out_weight = scatter_about(key_list[6], (D, D), D ** -0.5, 0.09375, ((0, 32), (1, 4)))
    return dict(query_rows=query_rows, key_rows=key_rows, value_rows=value_rows, residue=residue, pole_rate=pole_rate, skip_gain=skip_gain, out_weight=out_weight)


def filter_response(signal, residue, pole_rate):
    decay_rate = pole_rate / L
    weight = residue * jnp.sqrt(2.0 * decay_rate)
    lag_values = jnp.arange(L, dtype=jnp.float32)[:, None]
    filter_taps = jnp.zeros(signal.shape, jnp.float32)
    for pole_index in range(ORDER):
        filter_taps = filter_taps + weight[:, pole_index][None, :] * jnp.exp(-decay_rate[:, pole_index][None, :] * lag_values)
    padded_len = 2 * L
    spectrum = jnp.fft.rfft(filter_taps, n=padded_len, axis=0) * jnp.fft.rfft(signal, n=padded_len, axis=0)
    return jnp.fft.irfft(spectrum, n=padded_len, axis=0)[:L]

def reference(query_rows, key_rows, value_rows, residue, pole_rate, skip_gain, out_weight):
    product = lax.optimization_barrier((key_rows.astype(jnp.float32) * value_rows.astype(jnp.float32)).astype(jnp.bfloat16))
    signal = product.astype(jnp.float32)
    group_width = math.gcd(D, 256)
    group_count = D // group_width
    grouped = signal.reshape(L, group_count, group_width).transpose(1, 0, 2)
    residue_groups = residue.reshape(group_count, group_width, ORDER)
    rate_groups = pole_rate.reshape(group_count, group_width, ORDER)
    convolved = lax.map(lambda parts: filter_response(parts[0], parts[1], parts[2]), (grouped, residue_groups, rate_groups))
    convolved = convolved.transpose(1, 0, 2).reshape(L, D)
    mixed = lax.optimization_barrier((convolved + skip_gain[None, :] * signal).astype(jnp.bfloat16))
    gated = (query_rows.astype(jnp.float32) * mixed.astype(jnp.float32)).astype(jnp.bfloat16)
    projected = jnp.dot(gated, out_weight, preferred_element_type=jnp.float32).astype(jnp.bfloat16)
    return projected.reshape(N_SEQ, TOK_SEQ, D)
```

```python
import functools

import jax
import jax.numpy as jnp
from jax import lax
from jax.experimental import pallas as pl
from jax.experimental.pallas import tpu as pltpu
from jax.sharding import PartitionSpec as P

ORDER = 16
LANES = 128
ROWS = 8
UNROLL = 8
CHUNKS = 4
VMEM_LIMIT = 32 * 1024 * 1024


def states_kernel(rate_ref, key_ref, value_ref, signal_ref, state_ref):
    tokens = key_ref.shape[0]
    product = key_ref[...].astype(jnp.float32) * value_ref[...].astype(jnp.float32)
    product = product.astype(jnp.bfloat16).astype(jnp.float32)
    for j in range(ROWS):
        signal_ref[pl.ds(j, tokens, stride=ROWS), :] = product[:, j * LANES : (j + 1) * LANES]
    retain = [jnp.exp(-rate_ref[m]) for m in range(ORDER)]

    def several(step, held):
        for u in range(UNROLL):
            at = pl.multiple_of((step * UNROLL + u) * ROWS, ROWS)
            now = signal_ref[pl.ds(at, ROWS), :]
            held = [retain[m] * held[m] + now for m in range(ORDER)]
        return held

    zero = jnp.zeros((ROWS, LANES), jnp.float32)
    held = lax.fori_loop(0, tokens // UNROLL, several, [zero] * ORDER)
    for m in range(ORDER):
        state_ref[m] = held[m]


def tree_sum(terms):
    while len(terms) > 1:
        terms = [a + b for a, b in zip(terms[::2], terms[1::2])] + terms[len(terms) & ~1 :]
    return terms[0]


def local_kernel(param_ref, signal_ref, local_ref):
    tokens = signal_ref.shape[0] // ROWS
    retain = [jnp.exp(-param_ref[m]) for m in range(ORDER)]
    weight = [param_ref[ORDER + m] for m in range(ORDER)]
    skip = param_ref[2 * ORDER]

    def several(step, held):
        for u in range(UNROLL):
            at = pl.multiple_of((step * UNROLL + u) * ROWS, ROWS)
            now = signal_ref[pl.ds(at, ROWS), :]
            held = [retain[m] * held[m] + now for m in range(ORDER)]
            local_ref[pl.ds(at, ROWS), :] = (
                tree_sum([weight[m] * held[m] for m in range(ORDER)]) + skip * now
            )
        return held

    zero = jnp.zeros((ROWS, LANES), jnp.float32)
    lax.fori_loop(0, tokens // UNROLL, several, [zero] * ORDER)


def gate_kernel(param_ref, before_ref, local_ref, query_ref, gated_ref, mixed_ref):
    tokens = query_ref.shape[0]
    retain = [jnp.exp(-param_ref[m]) for m in range(ORDER)]
    start = [param_ref[ORDER + m] * before_ref[m] for m in range(ORDER)]

    def several(step, held):
        for u in range(UNROLL):
            at = pl.multiple_of((step * UNROLL + u) * ROWS, ROWS)
            held = [retain[m] * held[m] for m in range(ORDER)]
            mixed_ref[pl.ds(at, ROWS), :] = local_ref[pl.ds(at, ROWS), :] + tree_sum(held)
        return held

    lax.fori_loop(0, tokens // UNROLL, several, start)
    for j in range(ROWS):
        mixed = mixed_ref[pl.ds(j, tokens, stride=ROWS), :].astype(jnp.bfloat16)
        columns = slice(j * LANES, (j + 1) * LANES)
        gated = query_ref[:, columns].astype(jnp.float32) * mixed.astype(jnp.float32)
        gated_ref[:, columns] = gated.astype(jnp.bfloat16)


def compiler_params():
    return pltpu.CompilerParams(vmem_limit_bytes=VMEM_LIMIT)


def block_states(params, key_rows, value_rows):
    tokens, width = key_rows.shape
    groups = width // (ROWS * LANES)
    count = tokens * width * ORDER
    return pl.pallas_call(
        states_kernel,
        grid=(groups,),
        in_specs=[
            pl.BlockSpec((ORDER, ROWS, LANES), lambda g: (0, g, 0)),
            pl.BlockSpec((tokens, ROWS * LANES), lambda g: (0, g)),
            pl.BlockSpec((tokens, ROWS * LANES), lambda g: (0, g)),
        ],
        out_specs=[
            pl.BlockSpec((None, tokens * ROWS, LANES), lambda g: (g, 0, 0)),
            pl.BlockSpec((ORDER, ROWS, LANES), lambda g: (0, g, 0)),
        ],
        out_shape=[
            jax.ShapeDtypeStruct((groups, tokens * ROWS, LANES), jnp.float32),
            jax.ShapeDtypeStruct((ORDER, width // LANES, LANES), jnp.float32),
        ],
        compiler_params=compiler_params(),
        cost_estimate=pl.CostEstimate(flops=2 * count, bytes_accessed=8 * tokens * width, transcendentals=0),
        name="block_states",
    )(params, key_rows, value_rows)


def local_part(params, signal):
    groups, rows, _ = signal.shape
    count = groups * rows * LANES
    return pl.pallas_call(
        local_kernel,
        grid=(groups,),
        in_specs=[
            pl.BlockSpec((2 * ORDER + 1, ROWS, LANES), lambda g: (0, g, 0)),
            pl.BlockSpec((None, rows, LANES), lambda g: (g, 0, 0)),
        ],
        out_specs=pl.BlockSpec((None, rows, LANES), lambda g: (g, 0, 0)),
        out_shape=jax.ShapeDtypeStruct(signal.shape, jnp.float32),
        compiler_params=compiler_params(),
        cost_estimate=pl.CostEstimate(flops=4 * ORDER * count, bytes_accessed=8 * count, transcendentals=0),
        name="local_part",
    )(params, signal)


def gate_part(params, before, local, query_rows, first, count):
    tokens = query_rows.shape[0]
    size = tokens * ROWS * LANES * count
    return pl.pallas_call(
        gate_kernel,
        grid=(count,),
        in_specs=[
            pl.BlockSpec((2 * ORDER + 1, ROWS, LANES), lambda g: (0, g + first, 0)),
            pl.BlockSpec((ORDER, ROWS, LANES), lambda g: (0, g + first, 0)),
            pl.BlockSpec((None, tokens * ROWS, LANES), lambda g: (g + first, 0, 0)),
            pl.BlockSpec((tokens, ROWS * LANES), lambda g: (0, g + first)),
        ],
        out_specs=pl.BlockSpec((tokens, ROWS * LANES), lambda g: (0, g)),
        out_shape=jax.ShapeDtypeStruct((tokens, ROWS * LANES * count), jnp.bfloat16),
        scratch_shapes=[pltpu.VMEM((tokens * ROWS, LANES), jnp.float32)],
        compiler_params=compiler_params(),
        cost_estimate=pl.CostEstimate(flops=2 * ORDER * size, bytes_accessed=8 * size, transcendentals=0),
        name="gate_part",
    )(params, before, local, query_rows)


def combine(own, received, place, members, rate, span):
    position = place.astype(jnp.float32)
    decay = rate * float(span)
    total = jnp.exp(-decay * (members - 1 - position)) * own
    prefix = jnp.zeros_like(own)
    for s, other in enumerate(received, 1):
        other = other.astype(jnp.float32)
        earlier = place >= s
        power = jnp.where(earlier, members - 1 - position + s, s - 1 - position)
        total = total + jnp.exp(-decay * power) * other
        prefix = prefix + jnp.where(earlier, jnp.exp(-decay * (s - 1.0)) * other, 0.0)
    return total, prefix


def on_device(query_rows, key_rows, value_rows, residue, pole_rate, skip_gain, out_weight):
    tokens, width = query_rows.shape
    seq_count = lax.axis_size("seq")
    chan_count = lax.axis_size("chan")
    z, chan = lax.axis_index("seq"), lax.axis_index("chan")
    core, y, x = chan % 2, chan // 2 % 4, chan // 8
    length = tokens * seq_count * chan_count

    rate = pole_rate / length
    weight = residue * jnp.sqrt(2.0 * rate)
    own_params = jnp.concatenate([rate.T, weight.T, skip_gain[None, :]], axis=0)
    params = lax.all_gather(own_params, "chan", axis=1)
    full_weight = lax.all_gather(out_weight, "chan", axis=0, tiled=True)

    signal, state = block_states(params, key_rows, value_rows)
    local = local_part(params, signal)
    rates = params[:ORDER]

    def from_chan(array, shift):
        return lax.ppermute(array, "chan", [(i, shift(i)) for i in range(chan_count)])

    sent = state.astype(jnp.bfloat16)
    got = [from_chan(sent, lambda i: i ^ 1)]
    total, before = combine(state, got, core, 2, rates, tokens)

    sent = total.astype(jnp.bfloat16)
    got = [from_chan(sent, lambda i, s=s: i // 8 * 8 + (i + 2 * s) % 8) for s in (1, 2, 3)]
    total, prefix = combine(total, got, y, 4, rates, 2 * tokens)
    gone = (core * tokens).astype(jnp.float32)
    before = before + jnp.exp(-rates * gone) * prefix

    sent = total.astype(jnp.bfloat16)
    got = [from_chan(sent, lambda i, s=s: (i + 8 * s) % 32) for s in (1, 2, 3)]
    total, prefix = combine(total, got, x, 4, rates, 8 * tokens)
    gone = gone + (y * 2 * tokens).astype(jnp.float32)
    before = before + jnp.exp(-rates * gone) * prefix

    def from_seq(array, s):
        return lax.ppermute(array, "seq", [(i, (i + s) % seq_count) for i in range(seq_count)])

    sent = total.astype(jnp.bfloat16)
    got = [from_seq(sent, s) for s in (1, 2, 3)]
    _, prefix = combine(total, got, z, 4, rates, 32 * tokens)
    gone = gone + (x * 8 * tokens).astype(jnp.float32)
    before = before + jnp.exp(-rates * gone) * prefix

    groups = width // (ROWS * LANES)
    each = groups // CHUNKS
    half = tokens // 2
    sums = [None] * 4
    for c in range(CHUNKS):
        gated = gate_part(params, before, local, query_rows, c * each, each)
        rows = full_weight[c * each * ROWS * LANES : (c + 1) * each * ROWS * LANES]
        lower, upper = from_seq(gated, 1), from_seq(gated, -1)
        far_upper = from_seq(upper[half:], -1)
        far_lower = from_seq(lower[:half], 1)
        far = jnp.concatenate([far_lower, far_upper], axis=0)
        for n, part in enumerate((gated, upper, far, lower)):
            term = jnp.dot(part, rows, preferred_element_type=jnp.float32)
            sums[n] = term if sums[n] is None else sums[n] + term
    stacked = jnp.stack([s.astype(jnp.bfloat16) for s in sums])
    return jnp.roll(stacked, z, axis=0)


def solution(mesh):
    in_specs = (
        P(("seq", "chan"), None),
        P(("seq", "chan"), None),
        P(("seq", "chan"), None),
        P("chan", None),
        P("chan", None),
        P("chan"),
        P("chan", "seq"),
    )
    out_specs = P(None, "chan", "seq")
    return jax.shard_map(
        on_device, mesh=mesh, in_specs=in_specs, out_specs=out_specs, check_vma=False
    )
```

```python
import functools

import jax
import jax.numpy as jnp
from jax import lax
from jax.experimental import pallas as pl
from jax.experimental.pallas import tpu as pltpu
from jax.sharding import PartitionSpec as P

ORDER = 16
LANES = 128
ROWS = 8
GROUP = ROWS * LANES
UNROLL = 8
PARAMS = 5 * ORDER
SMALL_LIMIT = 16 * 1024 * 1024
LARGE_LIMIT = 56 * 1024 * 1024
COLUMNS = 256


def call(kernel, name, limit=SMALL_LIMIT, **keywords):
    return pl.pallas_call(
        kernel,
        name=name,
        compiler_params=pltpu.CompilerParams(vmem_limit_bytes=limit),
        cost_estimate=pl.CostEstimate(flops=1024, bytes_accessed=1024, transcendentals=0),
        **keywords,
    )


def as_float(block):
    return block.astype(jnp.float32)


def tree_sum(terms):
    while len(terms) > 1:
        terms = [a + b for a, b in zip(terms[::2], terms[1::2])] + terms[len(terms) & ~1 :]
    return terms[0]


def over_tokens(tokens, step, held):
    def several(outer, held):
        for u in range(UNROLL):
            held = step(pl.multiple_of((outer * UNROLL + u) * ROWS, ROWS), held)
        return held

    return lax.fori_loop(0, tokens // UNROLL, several, held)


def signal_kernel(key_ref, value_ref, signal_ref):
    signal = (as_float(key_ref[...]) * as_float(value_ref[...])).astype(jnp.bfloat16)
    for j in range(ROWS):
        signal_ref[j] = signal[:, j * LANES : (j + 1) * LANES]


def make_signal(key_rows, value_rows):
    tokens, width = key_rows.shape
    natural = pl.BlockSpec((tokens, GROUP), lambda g: (0, g))
    return call(
        signal_kernel,
        "signal",
        limit=LARGE_LIMIT,
        grid=(width // GROUP,),
        in_specs=[natural, natural],
        out_specs=pl.BlockSpec((ROWS, tokens, LANES), lambda g: (g, 0, 0)),
        out_shape=jax.ShapeDtypeStruct((width // LANES, tokens, LANES), jnp.bfloat16),
    )(key_rows, value_rows)


def states_kernel(tokens, rate_ref, signal_ref, prefix_ref, total_ref, work_ref, state_ref):
    for j in range(ROWS):
        work_ref[pl.ds(j, tokens, stride=ROWS), :] = as_float(signal_ref[j])
    rate = rate_ref[...]
    retain = [
        jnp.broadcast_to(jnp.exp(-rate[m : m + 1, :]), (ROWS, LANES)) for m in range(ORDER)
    ]

    def step(at, held):
        now = work_ref[pl.ds(at, ROWS), :]
        return [retain[m] * held[m] + now for m in range(ORDER)]

    held = over_tokens(tokens, step, [jnp.zeros((ROWS, LANES), jnp.float32)] * ORDER)
    for m in range(ORDER):
        state_ref[pl.ds(m, ROWS, stride=ORDER), :] = held[m]

    @pl.when(pl.program_id(0) == 0)
    def _():
        total_ref[...] = jnp.zeros_like(total_ref)

    decay = jnp.exp(-rate * float(tokens))
    before = total_ref[...]
    for j in range(ROWS):
        prefix_ref[j * ORDER : (j + 1) * ORDER, :] = before
        before = decay * before + state_ref[j * ORDER : (j + 1) * ORDER, :]
    total_ref[...] = before


def block_states(tokens, rate, received):
    blocks, _, lanes = received.shape
    return call(
        functools.partial(states_kernel, tokens),
        "block_states",
        grid=(blocks // ROWS,),
        in_specs=[
            pl.BlockSpec((ORDER, lanes), lambda g: (0, 0)),
            pl.BlockSpec((ROWS, tokens, lanes), lambda g: (g, 0, 0)),
        ],
        out_specs=[
            pl.BlockSpec((ROWS * ORDER, lanes), lambda g: (g, 0)),
            pl.BlockSpec((ORDER, lanes), lambda g: (0, 0)),
        ],
        out_shape=[
            jax.ShapeDtypeStruct((blocks * ORDER, lanes), jnp.float32),
            jax.ShapeDtypeStruct((ORDER, lanes), jnp.float32),
        ],
        scratch_shapes=[
            pltpu.VMEM((tokens * ROWS, lanes), jnp.float32),
            pltpu.VMEM((ROWS * ORDER, lanes), jnp.float32),
        ],
    )(rate, received)


def before_kernel(tokens, place_ref, rate_ref, weight_ref, skip_ref, prefix_ref, *refs):
    *total_refs, packed_ref = refs
    blocks = packed_ref.shape[0]
    rate = rate_ref[...]

    def pair(value):
        high = value.astype(jnp.bfloat16)
        return [high, (value - as_float(high)).astype(jnp.bfloat16)]

    skip = [as_float(part) for part in pair(skip_ref[...])]
    index = lax.broadcasted_iota(jnp.int32, (ORDER, LANES), 0)
    skip = jnp.where(index == 0, skip[0], jnp.where(index == 1, skip[1], 0.0))
    params = pair(rate) + pair(weight_ref[...]) + [skip.astype(jnp.bfloat16)]
    decay = jnp.exp(-rate * float(tokens))
    start = jnp.zeros((ORDER, LANES), jnp.float32)
    for s, total_ref in enumerate(total_refs, 1):
        passed = jnp.exp(-rate * float(tokens * blocks * (s - 1)))
        start = start + jnp.where(place_ref[0] >= s, passed * total_ref[...], 0.0)
    for i in range(blocks):
        for n, part in enumerate(params):
            packed_ref[i, n * ORDER : (n + 1) * ORDER, :] = part
        before = prefix_ref[i * ORDER : (i + 1) * ORDER, :] + start
        packed_ref[i, PARAMS:, :] = before.astype(jnp.bfloat16)
        start = decay * start


def states_before(tokens, z, rate, weight, skip, prefix, totals):
    whole = pl.BlockSpec(memory_space=pltpu.VMEM)
    return call(
        functools.partial(before_kernel, tokens),
        "states_before",
        in_specs=[pl.BlockSpec(memory_space=pltpu.SMEM)] + [whole] * (4 + len(totals)),
        out_specs=whole,
        out_shape=jax.ShapeDtypeStruct(
            (prefix.shape[0] // ORDER, PARAMS + ORDER, LANES), jnp.bfloat16
        ),
    )(z.reshape(1), rate, weight, skip, prefix, *totals)


def gate_kernel(packed_ref, before_ref, signal_ref, query_ref, gated_ref, part_ref, start_ref, work_ref):
    tokens = query_ref.shape[0]
    for j in range(ROWS):
        part_ref[j * PARAMS : (j + 1) * PARAMS, :] = as_float(packed_ref[j])
        start_ref[j * ORDER : (j + 1) * ORDER, :] = as_float(before_ref[j])
        work_ref[pl.ds(j, tokens, stride=ROWS), :] = as_float(signal_ref[j])

    def row(n):
        return part_ref[pl.ds(n, ROWS, stride=PARAMS), :]

    retain = [jnp.exp(-(row(m) + row(ORDER + m))) for m in range(ORDER)]
    weight = [row(2 * ORDER + m) + row(3 * ORDER + m) for m in range(ORDER)]
    skip = row(4 * ORDER) + row(4 * ORDER + 1)
    start = [start_ref[pl.ds(m, ROWS, stride=ORDER), :] for m in range(ORDER)]

    def step(at, held):
        now = work_ref[pl.ds(at, ROWS), :]
        held = [retain[m] * held[m] + now for m in range(ORDER)]
        terms = [weight[m] * held[m] for m in range(ORDER)]
        work_ref[pl.ds(at, ROWS), :] = tree_sum(terms) + skip * now
        return held

    over_tokens(tokens, step, start)
    for j in range(ROWS):
        mixed = work_ref[pl.ds(j, tokens, stride=ROWS), :].astype(jnp.bfloat16)
        columns = slice(j * LANES, (j + 1) * LANES)
        gated = as_float(query_ref[:, columns]) * as_float(mixed)
        gated_ref[:, columns] = gated.astype(jnp.bfloat16)


def gate_rows(packed, before, signal, query, first, count):
    tokens = query.shape[0]
    last = before.shape[1] // ORDER - 1
    return call(
        gate_kernel,
        "gate_rows",
        grid=(count,),
        in_specs=[
            pl.BlockSpec((ROWS, PARAMS, LANES), lambda g: (g + first, 0, 0)),
            pl.BlockSpec((ROWS, ORDER, LANES), lambda g: (g + first, last, 0)),
            pl.BlockSpec((ROWS, tokens, LANES), lambda g: (g + first, 0, 0)),
            pl.BlockSpec((tokens, GROUP), lambda g: (0, g + first)),
        ],
        out_specs=pl.BlockSpec((tokens, GROUP), lambda g: (0, g)),
        out_shape=jax.ShapeDtypeStruct((tokens, GROUP * count), jnp.bfloat16),
        scratch_shapes=[
            pltpu.VMEM((ROWS * PARAMS, LANES), jnp.float32),
            pltpu.VMEM((ROWS * ORDER, LANES), jnp.float32),
            pltpu.VMEM((tokens * ROWS, LANES), jnp.float32),
        ],
    )(packed, before, signal, query)


def whole_kernel(first_ref, second_ref, far_ref, matrix_ref, out_ref, rows_ref):
    tokens, split = first_ref.shape
    rows_ref[:tokens, :split] = first_ref[...]
    rows_ref[:tokens, split:] = second_ref[...]
    rows_ref[tokens:, :] = far_ref[...]
    for n in range(0, out_ref.shape[1], COLUMNS):
        columns = slice(n, n + COLUMNS)
        product = jnp.dot(rows_ref[...], matrix_ref[:, columns], preferred_element_type=jnp.float32)
        out_ref[:, columns] = product.astype(jnp.bfloat16)


def whole_rows(first, second, far, matrix):
    whole = pl.BlockSpec(memory_space=pltpu.VMEM)
    tokens, columns = far.shape[0], matrix.shape[1]
    return call(
        whole_kernel,
        "whole_rows",
        in_specs=[whole] * 4,
        out_specs=whole,
        out_shape=jax.ShapeDtypeStruct((2 * tokens, columns), jnp.bfloat16),
        scratch_shapes=[pltpu.VMEM((2 * tokens, far.shape[1]), jnp.bfloat16)],
    )(first, second, far, matrix)


def half_kernel(upper_ref, lower_ref, matrix_ref, sum_ref, rows_ref):
    tokens, depth = upper_ref.shape
    rows_ref[:tokens, :] = upper_ref[...]
    rows_ref[tokens:, :] = lower_ref[...]
    for n in range(0, sum_ref.shape[1], COLUMNS):
        columns = slice(n, n + COLUMNS)
        sum_ref[:, columns] = jnp.dot(
            rows_ref[...], matrix_ref[:depth, columns], preferred_element_type=jnp.float32
        )


def half_rows(upper, lower, matrix):
    whole = pl.BlockSpec(memory_space=pltpu.VMEM)
    tokens, depth = upper.shape
    return call(
        half_kernel,
        "half_rows",
        in_specs=[whole] * 3,
        out_specs=whole,
        out_shape=jax.ShapeDtypeStruct((2 * tokens, matrix.shape[1]), jnp.float32),
        scratch_shapes=[pltpu.VMEM((2 * tokens, depth), jnp.bfloat16)],
    )(upper, lower, matrix)


def finish_kernel(place_ref, done_ref, sum_ref, upper_ref, lower_ref, matrix_ref, out_ref, rows_ref):
    tokens, depth = upper_ref.shape
    rows_ref[:tokens, :] = upper_ref[...]
    rows_ref[tokens:, :] = lower_ref[...]
    own, up, far, low = [lax.rem(place_ref[0] + r, 4) for r in range(4)]
    out_ref[own] = done_ref[:tokens, :]
    out_ref[far] = done_ref[tokens:, :]
    for n in range(0, out_ref.shape[2], COLUMNS):
        columns = slice(n, n + COLUMNS)
        matrix = matrix_ref[matrix_ref.shape[0] - depth :, columns]
        product = jnp.dot(rows_ref[...], matrix, preferred_element_type=jnp.float32)
        total = (sum_ref[:, columns] + product).astype(jnp.bfloat16)
        out_ref[up, :, columns] = total[:tokens]
        out_ref[low, :, columns] = total[tokens:]


def finish(z, done, early_sum, upper, lower, matrix):
    tokens, depth = upper.shape
    whole = pl.BlockSpec(memory_space=pltpu.VMEM)
    return call(
        finish_kernel,
        "finish",
        in_specs=[pl.BlockSpec(memory_space=pltpu.SMEM)] + [whole] * 5,
        out_specs=whole,
        out_shape=jax.ShapeDtypeStruct((4, tokens, matrix.shape[1]), jnp.bfloat16),
        scratch_shapes=[pltpu.VMEM((2 * tokens, depth), jnp.bfloat16)],
    )(z.reshape(1), done, early_sum, upper, lower, matrix)


def on_device(query_rows, key_rows, value_rows, residue, pole_rate, skip_gain, out_weight):
    tokens, width = query_rows.shape
    seq_count = lax.axis_size("seq")
    length = tokens * seq_count * lax.axis_size("chan")
    z = lax.axis_index("seq")
    half = width // GROUP // 2

    def from_seq(array, s):
        return lax.ppermute(array, "seq", [(i, (i + s) % seq_count) for i in range(seq_count)])

    def to_owners(array):
        return lax.all_to_all(array, "chan", split_axis=0, concat_axis=0, tiled=True)

    rate = pole_rate / length
    weight = (residue * jnp.sqrt(2.0 * rate)).T
    rate = rate.T
    far_query = from_seq(query_rows, 2)
    signal = make_signal(key_rows, value_rows)
    received = to_owners(signal)
    received, far_query, out_weight = lax.optimization_barrier((received, far_query, out_weight))
    full_weight = lax.all_gather(out_weight, "chan", axis=0, tiled=True)

    prefix, total = block_states(tokens, rate, received)
    totals = [from_seq(total, s) for s in (1, 2, 3)]
    packed = states_before(tokens, z, rate, weight, skip_gain[None, :], prefix, totals)
    packed, signal = lax.optimization_barrier((packed, signal))
    far_signal = from_seq(signal, 2)
    packed = to_owners(packed)
    packed, far_signal = lax.optimization_barrier((packed, far_signal))

    far_before = from_seq(packed[:, PARAMS:], 2)
    first = gate_rows(packed, packed, signal, query_rows, 0, half)
    first, far_before = lax.optimization_barrier((first, far_before))
    low_first, up_first = from_seq(first, 1), from_seq(first, -1)
    second = gate_rows(packed, packed, signal, query_rows, half, half)
    low_second, up_second = from_seq(second, 1), from_seq(second, -1)
    far = gate_rows(packed, far_before, far_signal, far_query, 0, 2 * half)
    done = whole_rows(first, second, far, full_weight)
    early_sum = half_rows(up_first, low_first, full_weight)
    return finish(z, done, early_sum, up_second, low_second, full_weight)


def solution(mesh):
    in_specs = (
        P(("seq", "chan"), None),
        P(("seq", "chan"), None),
        P(("seq", "chan"), None),
        P("chan", None),
        P("chan", None),
        P("chan"),
        P("chan", "seq"),
    )
    out_specs = P(None, "chan", "seq")
    return jax.shard_map(
        on_device, mesh=mesh, in_specs=in_specs, out_specs=out_specs, check_vma=False
    )
```

```python
import functools

import jax
import jax.numpy as jnp
from jax import lax
from jax.experimental import pallas as pl
from jax.experimental.pallas import tpu as pltpu
from jax.sharding import PartitionSpec as P

ORDER = 16
LANES = 128
ROWS = 8
GROUP = ROWS * LANES
UNROLL = 8
SLICE = 32
PARAMS = 5 * ORDER
SMALL_LIMIT = 16 * 1024 * 1024
LARGE_LIMIT = 56 * 1024 * 1024
COLUMNS = 256


def call(kernel, name, limit=SMALL_LIMIT, moved=1024, **keywords):
    return pl.pallas_call(
        kernel,
        name=name,
        compiler_params=pltpu.CompilerParams(vmem_limit_bytes=limit),
        cost_estimate=pl.CostEstimate(flops=1024, bytes_accessed=moved, transcendentals=0),
        **keywords,
    )


def as_float(block):
    return block.astype(jnp.float32)


def tree_sum(terms):
    while len(terms) > 1:
        terms = [a + b for a, b in zip(terms[::2], terms[1::2])] + terms[len(terms) & ~1 :]
    return terms[0]


def over_tokens(tokens, step, held):
    def several(outer, held):
        for u in range(UNROLL):
            held = step(pl.multiple_of((outer * UNROLL + u) * ROWS, ROWS), held)
        return held

    return lax.fori_loop(0, tokens // UNROLL, several, held)


def signal_kernel(key_hbm, value_hbm, signal_ref, key_ref, value_ref, sems):
    parts = sems.shape[1]
    size = key_ref.shape[0] // parts
    copies = []
    for n in range(parts):
        rows = pl.ds(n * size, size)
        for at, (source, target) in enumerate([(key_hbm, key_ref), (value_hbm, value_ref)]):
            copies.append(pltpu.make_async_copy(source.at[rows, :], target.at[rows, :], sems.at[at, n]))
            copies[-1].start()
    for n in range(parts):
        copies[2 * n].wait()
        copies[2 * n + 1].wait()
        rows = slice(n * size, (n + 1) * size)
        for j in range(signal_ref.shape[0]):
            columns = slice(j * LANES, (j + 1) * LANES)
            product = as_float(key_ref[rows, columns]) * as_float(value_ref[rows, columns])
            signal_ref[j, rows, :] = product.astype(jnp.bfloat16)


def make_signal(key_rows, value_rows):
    tokens, width = key_rows.shape
    outside = pl.BlockSpec(memory_space=pltpu.HBM)
    return call(
        signal_kernel,
        "signal",
        in_specs=[outside, outside],
        out_specs=pl.BlockSpec(memory_space=pltpu.VMEM),
        out_shape=jax.ShapeDtypeStruct((width // LANES, tokens, LANES), jnp.bfloat16),
        scratch_shapes=[
            pltpu.VMEM((tokens, width), jnp.bfloat16),
            pltpu.VMEM((tokens, width), jnp.bfloat16),
            pltpu.SemaphoreType.DMA((2, tokens // SLICE)),
        ],
    )(key_rows, value_rows)


def states_kernel(tokens, rate_ref, signal_ref, prefix_ref, total_ref, work_ref, state_ref):
    for j in range(ROWS):
        work_ref[pl.ds(j, tokens, stride=ROWS), :] = as_float(signal_ref[j])
    rate = rate_ref[...]
    retain = [
        jnp.broadcast_to(jnp.exp(-rate[m : m + 1, :]), (ROWS, LANES)) for m in range(ORDER)
    ]

    def step(at, held):
        now = work_ref[pl.ds(at, ROWS), :]
        return [retain[m] * held[m] + now for m in range(ORDER)]

    held = over_tokens(tokens, step, [jnp.zeros((ROWS, LANES), jnp.float32)] * ORDER)
    for m in range(ORDER):
        state_ref[pl.ds(m, ROWS, stride=ORDER), :] = held[m]

    @pl.when(pl.program_id(0) == 0)
    def _():
        total_ref[...] = jnp.zeros_like(total_ref)

    decay = jnp.exp(-rate * float(tokens))
    before = total_ref[...]
    for j in range(ROWS):
        prefix_ref[j * ORDER : (j + 1) * ORDER, :] = before
        before = decay * before + state_ref[j * ORDER : (j + 1) * ORDER, :]
    total_ref[...] = before


def block_states(tokens, rate, received):
    blocks, _, lanes = received.shape
    return call(
        functools.partial(states_kernel, tokens),
        "block_states",
        grid=(blocks // ROWS,),
        in_specs=[
            pl.BlockSpec((ORDER, lanes), lambda g: (0, 0)),
            pl.BlockSpec((ROWS, tokens, lanes), lambda g: (g, 0, 0)),
        ],
        out_specs=[
            pl.BlockSpec((ROWS * ORDER, lanes), lambda g: (g, 0)),
            pl.BlockSpec((ORDER, lanes), lambda g: (0, 0)),
        ],
        out_shape=[
            jax.ShapeDtypeStruct((blocks * ORDER, lanes), jnp.float32),
            jax.ShapeDtypeStruct((ORDER, lanes), jnp.float32),
        ],
        scratch_shapes=[
            pltpu.VMEM((tokens * ROWS, lanes), jnp.float32),
            pltpu.VMEM((ROWS * ORDER, lanes), jnp.float32),
        ],
    )(rate, received)


def before_kernel(tokens, place_ref, rate_ref, weight_ref, skip_ref, prefix_ref, *refs):
    *total_refs, packed_ref = refs
    blocks = packed_ref.shape[0]
    rate = rate_ref[...]

    def pair(value):
        high = value.astype(jnp.bfloat16)
        return [high, (value - as_float(high)).astype(jnp.bfloat16)]

    skip = [as_float(part) for part in pair(skip_ref[...])]
    index = lax.broadcasted_iota(jnp.int32, (ORDER, LANES), 0)
    skip = jnp.where(index == 0, skip[0], jnp.where(index == 1, skip[1], 0.0))
    params = pair(rate) + pair(weight_ref[...]) + [skip.astype(jnp.bfloat16)]
    decay = jnp.exp(-rate * float(tokens))
    start = jnp.zeros((ORDER, LANES), jnp.float32)
    for s, total_ref in enumerate(total_refs, 1):
        passed = jnp.exp(-rate * float(tokens * blocks * (s - 1)))
        start = start + jnp.where(place_ref[0] >= s, passed * total_ref[...], 0.0)
    for i in range(blocks):
        for n, part in enumerate(params):
            packed_ref[i, n * ORDER : (n + 1) * ORDER, :] = part
        before = prefix_ref[i * ORDER : (i + 1) * ORDER, :] + start
        packed_ref[i, PARAMS:, :] = before.astype(jnp.bfloat16)
        start = decay * start


def states_before(tokens, z, rate, weight, skip, prefix, totals):
    whole = pl.BlockSpec(memory_space=pltpu.VMEM)
    return call(
        functools.partial(before_kernel, tokens),
        "states_before",
        in_specs=[pl.BlockSpec(memory_space=pltpu.SMEM)] + [whole] * (4 + len(totals)),
        out_specs=whole,
        out_shape=jax.ShapeDtypeStruct(
            (prefix.shape[0] // ORDER, PARAMS + ORDER, LANES), jnp.bfloat16
        ),
    )(z.reshape(1), rate, weight, skip, prefix, *totals)


def gate_kernel(packed_ref, before_ref, signal_ref, query_ref, gated_ref, part_ref, start_ref, work_ref):
    tokens = query_ref.shape[0]
    for j in range(ROWS):
        part_ref[j * PARAMS : (j + 1) * PARAMS, :] = as_float(packed_ref[j])
        start_ref[j * ORDER : (j + 1) * ORDER, :] = as_float(before_ref[j])
        work_ref[pl.ds(j, tokens, stride=ROWS), :] = as_float(signal_ref[j])

    def row(n):
        return part_ref[pl.ds(n, ROWS, stride=PARAMS), :]

    retain = [jnp.exp(-(row(m) + row(ORDER + m))) for m in range(ORDER)]
    weight = [row(2 * ORDER + m) + row(3 * ORDER + m) for m in range(ORDER)]
    skip = row(4 * ORDER) + row(4 * ORDER + 1)
    start = [start_ref[pl.ds(m, ROWS, stride=ORDER), :] for m in range(ORDER)]

    def step(at, held):
        now = work_ref[pl.ds(at, ROWS), :]
        held = [retain[m] * held[m] + now for m in range(ORDER)]
        terms = [weight[m] * held[m] for m in range(ORDER)]
        work_ref[pl.ds(at, ROWS), :] = tree_sum(terms) + skip * now
        return held

    over_tokens(tokens, step, start)
    for j in range(ROWS):
        mixed = work_ref[pl.ds(j, tokens, stride=ROWS), :].astype(jnp.bfloat16)
        columns = slice(j * LANES, (j + 1) * LANES)
        gated = as_float(query_ref[:, columns]) * as_float(mixed)
        gated_ref[:, columns] = gated.astype(jnp.bfloat16)


def gate_rows(packed, before, signal, query, first, count, moved=1024):
    tokens = query.shape[0]
    last = before.shape[1] // ORDER - 1
    return call(
        gate_kernel,
        "gate_rows",
        moved=moved,
        grid=(count,),
        in_specs=[
            pl.BlockSpec((ROWS, PARAMS, LANES), lambda g: (g + first, 0, 0)),
            pl.BlockSpec((ROWS, ORDER, LANES), lambda g: (g + first, last, 0)),
            pl.BlockSpec((ROWS, tokens, LANES), lambda g: (g + first, 0, 0)),
            pl.BlockSpec((tokens, GROUP), lambda g: (0, g + first)),
        ],
        out_specs=pl.BlockSpec((tokens, GROUP), lambda g: (0, g)),
        out_shape=jax.ShapeDtypeStruct((tokens, GROUP * count), jnp.bfloat16),
        scratch_shapes=[
            pltpu.VMEM((ROWS * PARAMS, LANES), jnp.float32),
            pltpu.VMEM((ROWS * ORDER, LANES), jnp.float32),
            pltpu.VMEM((tokens * ROWS, LANES), jnp.float32),
        ],
    )(packed, before, signal, query)


def early_kernel(first_ref, second_ref, far_ref, upper_ref, lower_ref, matrix_ref, done_ref, sum_ref, rows_ref, half_ref):
    tokens, split = first_ref.shape
    rows_ref[:tokens, :split] = first_ref[...]
    rows_ref[:tokens, split:] = second_ref[...]
    rows_ref[tokens:, :] = far_ref[...]
    half_ref[:tokens, :] = upper_ref[...]
    half_ref[tokens:, :] = lower_ref[...]
    for n in range(0, done_ref.shape[1], COLUMNS):
        columns = slice(n, n + COLUMNS)
        product = jnp.dot(rows_ref[...], matrix_ref[:, columns], preferred_element_type=jnp.float32)
        done_ref[:, columns] = product.astype(jnp.bfloat16)
        sum_ref[:, columns] = jnp.dot(
            half_ref[...], matrix_ref[:split, columns], preferred_element_type=jnp.float32
        )


def early_rows(first, second, far, upper, lower, matrix):
    whole = pl.BlockSpec(memory_space=pltpu.VMEM)
    tokens, columns = far.shape[0], matrix.shape[1]
    return call(
        early_kernel,
        "early_rows",
        in_specs=[whole] * 6,
        out_specs=[whole] * 2,
        out_shape=[
            jax.ShapeDtypeStruct((2 * tokens, columns), jnp.bfloat16),
            jax.ShapeDtypeStruct((2 * tokens, columns), jnp.float32),
        ],
        scratch_shapes=[
            pltpu.VMEM((2 * tokens, far.shape[1]), jnp.bfloat16),
            pltpu.VMEM((2 * tokens, first.shape[1]), jnp.bfloat16),
        ],
    )(first, second, far, upper, lower, matrix)


def finish_kernel(place_ref, done_ref, sum_ref, upper_ref, lower_ref, matrix_ref, out_ref, rows_ref):
    tokens, depth = upper_ref.shape
    rows_ref[:tokens, :] = upper_ref[...]
    rows_ref[tokens:, :] = lower_ref[...]
    own, up, far, low = [lax.rem(place_ref[0] + r, 4) for r in range(4)]
    out_ref[own] = done_ref[:tokens, :]
    out_ref[far] = done_ref[tokens:, :]
    for n in range(0, out_ref.shape[2], COLUMNS):
        columns = slice(n, n + COLUMNS)
        matrix = matrix_ref[matrix_ref.shape[0] - depth :, columns]
        product = jnp.dot(rows_ref[...], matrix, preferred_element_type=jnp.float32)
        total = (sum_ref[:, columns] + product).astype(jnp.bfloat16)
        out_ref[up, :, columns] = total[:tokens]
        out_ref[low, :, columns] = total[tokens:]


def finish(z, done, early_sum, upper, lower, matrix):
    tokens, depth = upper.shape
    whole = pl.BlockSpec(memory_space=pltpu.VMEM)
    return call(
        finish_kernel,
        "finish",
        in_specs=[pl.BlockSpec(memory_space=pltpu.SMEM)] + [whole] * 5,
        out_specs=whole,
        out_shape=jax.ShapeDtypeStruct((4, tokens, matrix.shape[1]), jnp.bfloat16),
        scratch_shapes=[pltpu.VMEM((2 * tokens, depth), jnp.bfloat16)],
    )(z.reshape(1), done, early_sum, upper, lower, matrix)


def on_device(query_rows, key_rows, value_rows, residue, pole_rate, skip_gain, out_weight):
    tokens, width = query_rows.shape
    seq_count = lax.axis_size("seq")
    length = tokens * seq_count * lax.axis_size("chan")
    z = lax.axis_index("seq")
    half = width // GROUP // 2

    def from_seq(array, s):
        return lax.ppermute(array, "seq", [(i, (i + s) % seq_count) for i in range(seq_count)])

    def to_owners(array):
        return lax.all_to_all(array, "chan", split_axis=0, concat_axis=0, tiled=True)

    rate = pole_rate / length
    weight = (residue * jnp.sqrt(2.0 * rate)).T
    rate = rate.T
    far_query = from_seq(query_rows, 2)
    signal = make_signal(key_rows, value_rows)
    received = to_owners(signal)
    received, far_query, out_weight = lax.optimization_barrier((received, far_query, out_weight))
    full_weight = lax.all_gather(out_weight, "chan", axis=0, tiled=True)

    prefix, total = block_states(tokens, rate, received)
    totals = [from_seq(total, s) for s in (1, 2, 3)]
    totals, signal = lax.optimization_barrier((totals, signal))
    far_signal = from_seq(signal, 2)
    packed = states_before(tokens, z, rate, weight, skip_gain[None, :], prefix, totals)
    packed = to_owners(packed)
    far_before = from_seq(packed[:, PARAMS:], 2)
    first = gate_rows(packed, packed, signal, query_rows, 0, half)
    first, far_before, far_signal = lax.optimization_barrier((first, far_before, far_signal))
    low_first, up_first = from_seq(first, 1), from_seq(first, -1)
    second = gate_rows(packed, packed, signal, query_rows, half, half)
    low_second, up_second = from_seq(second, 1), from_seq(second, -1)
    second, far_before = lax.optimization_barrier((second, far_before))
    far = gate_rows(packed, far_before, far_signal, far_query, 0, 2 * half, 20 * 1024 * 1024)
    done, early_sum = early_rows(first, second, far, up_first, low_first, full_weight)
    return finish(z, done, early_sum, up_second, low_second, full_weight)


def solution(mesh):
    in_specs = (
        P(("seq", "chan"), None),
        P(("seq", "chan"), None),
        P(("seq", "chan"), None),
        P("chan", None),
        P("chan", None),
        P("chan"),
        P("chan", "seq"),
    )
    out_specs = P(None, "chan", "seq")
    return jax.shard_map(
        on_device, mesh=mesh, in_specs=in_specs, out_specs=out_specs, check_vma=False
    )
```

```python
import functools

import jax
import jax.numpy as jnp
from jax import lax
from jax.experimental import pallas as pl
from jax.experimental.pallas import tpu as pltpu
from jax.sharding import PartitionSpec as P

ORDER = 16
LANES = 128
ROWS = 8
GROUP = ROWS * LANES
UNROLL = 8
SLICE = 32
PARAMS = 5 * ORDER
SMALL_LIMIT = 16 * 1024 * 1024
LARGE_LIMIT = 56 * 1024 * 1024
COLUMNS = 256


def call(kernel, name, limit=SMALL_LIMIT, moved=1024, **keywords):
    return pl.pallas_call(
        kernel,
        name=name,
        compiler_params=pltpu.CompilerParams(vmem_limit_bytes=limit),
        cost_estimate=pl.CostEstimate(flops=1024, bytes_accessed=moved, transcendentals=0),
        **keywords,
    )


def as_float(block):
    return block.astype(jnp.float32)


def tree_sum(terms):
    while len(terms) > 1:
        terms = [a + b for a, b in zip(terms[::2], terms[1::2])] + terms[len(terms) & ~1 :]
    return terms[0]


def over_tokens(tokens, step, held):
    def several(outer, held):
        for u in range(UNROLL):
            held = step(pl.multiple_of((outer * UNROLL + u) * ROWS, ROWS), held)
        return held

    return lax.fori_loop(0, tokens // UNROLL, several, held)


def signal_kernel(key_hbm, value_hbm, signal_ref, key_ref, value_ref, sems):
    parts = sems.shape[1]
    size = key_ref.shape[0] // parts
    copies = []
    for n in range(parts):
        rows = pl.ds(n * size, size)
        for at, (source, target) in enumerate([(key_hbm, key_ref), (value_hbm, value_ref)]):
            copies.append(pltpu.make_async_copy(source.at[rows, :], target.at[rows, :], sems.at[at, n]))
            copies[-1].start()
    for n in range(parts):
        copies[2 * n].wait()
        copies[2 * n + 1].wait()
        rows = slice(n * size, (n + 1) * size)
        for j in range(signal_ref.shape[0]):
            columns = slice(j * LANES, (j + 1) * LANES)
            product = as_float(key_ref[rows, columns]) * as_float(value_ref[rows, columns])
            signal_ref[j, rows, :] = product.astype(jnp.bfloat16)


def make_signal(key_rows, value_rows):
    tokens, width = key_rows.shape
    outside = pl.BlockSpec(memory_space=pltpu.HBM)
    return call(
        signal_kernel,
        "signal",
        in_specs=[outside, outside],
        out_specs=pl.BlockSpec(memory_space=pltpu.VMEM),
        out_shape=jax.ShapeDtypeStruct((width // LANES, tokens, LANES), jnp.bfloat16),
        scratch_shapes=[
            pltpu.VMEM((tokens, width), jnp.bfloat16),
            pltpu.VMEM((tokens, width), jnp.bfloat16),
            pltpu.SemaphoreType.DMA((2, tokens // SLICE)),
        ],
    )(key_rows, value_rows)


def states_kernel(tokens, rate_ref, signal_ref, prefix_ref, total_ref, work_ref, state_ref):
    for j in range(ROWS):
        work_ref[pl.ds(j, tokens, stride=ROWS), :] = as_float(signal_ref[j])
    rate = rate_ref[...]
    retain = [
        jnp.broadcast_to(jnp.exp(-rate[m : m + 1, :]), (ROWS, LANES)) for m in range(ORDER)
    ]

    def step(at, held):
        now = work_ref[pl.ds(at, ROWS), :]
        return [retain[m] * held[m] + now for m in range(ORDER)]

    held = over_tokens(tokens, step, [jnp.zeros((ROWS, LANES), jnp.float32)] * ORDER)
    for m in range(ORDER):
        state_ref[pl.ds(m, ROWS, stride=ORDER), :] = held[m]

    @pl.when(pl.program_id(0) == 0)
    def _():
        total_ref[...] = jnp.zeros_like(total_ref)

    decay = jnp.exp(-rate * float(tokens))
    before = total_ref[...]
    for j in range(ROWS):
        prefix_ref[j * ORDER : (j + 1) * ORDER, :] = before
        before = decay * before + state_ref[j * ORDER : (j + 1) * ORDER, :]
    total_ref[...] = before


def block_states(tokens, rate, received):
    blocks, _, lanes = received.shape
    return call(
        functools.partial(states_kernel, tokens),
        "block_states",
        grid=(blocks // ROWS,),
        in_specs=[
            pl.BlockSpec((ORDER, lanes), lambda g: (0, 0)),
            pl.BlockSpec((ROWS, tokens, lanes), lambda g: (g, 0, 0)),
        ],
        out_specs=[
            pl.BlockSpec((ROWS * ORDER, lanes), lambda g: (g, 0)),
            pl.BlockSpec((ORDER, lanes), lambda g: (0, 0)),
        ],
        out_shape=[
            jax.ShapeDtypeStruct((blocks * ORDER, lanes), jnp.float32),
            jax.ShapeDtypeStruct((ORDER, lanes), jnp.float32),
        ],
        scratch_shapes=[
            pltpu.VMEM((tokens * ROWS, lanes), jnp.float32),
            pltpu.VMEM((ROWS * ORDER, lanes), jnp.float32),
        ],
    )(rate, received)


def before_kernel(tokens, place_ref, rate_ref, weight_ref, skip_ref, prefix_ref, *refs):
    *total_refs, packed_ref = refs
    blocks = packed_ref.shape[0]
    rate = rate_ref[...]

    def pair(value):
        high = value.astype(jnp.bfloat16)
        return [high, (value - as_float(high)).astype(jnp.bfloat16)]

    skip = [as_float(part) for part in pair(skip_ref[...])]
    index = lax.broadcasted_iota(jnp.int32, (ORDER, LANES), 0)
    skip = jnp.where(index == 0, skip[0], jnp.where(index == 1, skip[1], 0.0))
    params = pair(rate) + pair(weight_ref[...]) + [skip.astype(jnp.bfloat16)]
    decay = jnp.exp(-rate * float(tokens))
    start = jnp.zeros((ORDER, LANES), jnp.float32)
    for s, total_ref in enumerate(total_refs, 1):
        passed = jnp.exp(-rate * float(tokens * blocks * (s - 1)))
        start = start + jnp.where(place_ref[0] >= s, passed * total_ref[...], 0.0)
    for i in range(blocks):
        for n, part in enumerate(params):
            packed_ref[i, n * ORDER : (n + 1) * ORDER, :] = part
        before = prefix_ref[i * ORDER : (i + 1) * ORDER, :] + start
        packed_ref[i, PARAMS:, :] = before.astype(jnp.bfloat16)
        start = decay * start


def states_before(tokens, z, rate, weight, skip, prefix, totals):
    whole = pl.BlockSpec(memory_space=pltpu.VMEM)
    return call(
        functools.partial(before_kernel, tokens),
        "states_before",
        in_specs=[pl.BlockSpec(memory_space=pltpu.SMEM)] + [whole] * (4 + len(totals)),
        out_specs=whole,
        out_shape=jax.ShapeDtypeStruct(
            (prefix.shape[0] // ORDER, PARAMS + ORDER, LANES), jnp.bfloat16
        ),
    )(z.reshape(1), rate, weight, skip, prefix, *totals)


def gate_kernel(packed_ref, before_ref, signal_ref, query_ref, gated_ref, part_ref, start_ref, work_ref):
    tokens = query_ref.shape[0]
    for j in range(ROWS):
        part_ref[j * PARAMS : (j + 1) * PARAMS, :] = as_float(packed_ref[j])
        start_ref[j * ORDER : (j + 1) * ORDER, :] = as_float(before_ref[j])
        work_ref[pl.ds(j, tokens, stride=ROWS), :] = as_float(signal_ref[j])

    def row(n):
        return part_ref[pl.ds(n, ROWS, stride=PARAMS), :]

    retain = [jnp.exp(-(row(m) + row(ORDER + m))) for m in range(ORDER)]
    weight = [row(2 * ORDER + m) + row(3 * ORDER + m) for m in range(ORDER)]
    skip = row(4 * ORDER) + row(4 * ORDER + 1)
    start = [start_ref[pl.ds(m, ROWS, stride=ORDER), :] for m in range(ORDER)]

    def step(at, held):
        now = work_ref[pl.ds(at, ROWS), :]
        held = [retain[m] * held[m] + now for m in range(ORDER)]
        terms = [weight[m] * held[m] for m in range(ORDER)]
        work_ref[pl.ds(at, ROWS), :] = tree_sum(terms) + skip * now
        return held

    over_tokens(tokens, step, start)
    for j in range(ROWS):
        mixed = work_ref[pl.ds(j, tokens, stride=ROWS), :].astype(jnp.bfloat16)
        columns = slice(j * LANES, (j + 1) * LANES)
        gated = as_float(query_ref[:, columns]) * as_float(mixed)
        gated_ref[:, columns] = gated.astype(jnp.bfloat16)


def gate_rows(packed, before, signal, query, first, count, moved=1024):
    tokens = query.shape[0]
    last = before.shape[1] // ORDER - 1
    return call(
        gate_kernel,
        "gate_rows",
        moved=moved,
        grid=(count,),
        in_specs=[
            pl.BlockSpec((ROWS, PARAMS, LANES), lambda g: (g + first, 0, 0)),
            pl.BlockSpec((ROWS, ORDER, LANES), lambda g: (g + first, last, 0)),
            pl.BlockSpec((ROWS, tokens, LANES), lambda g: (g + first, 0, 0)),
            pl.BlockSpec((tokens, GROUP), lambda g: (0, g + first)),
        ],
        out_specs=pl.BlockSpec((tokens, GROUP), lambda g: (0, g)),
        out_shape=jax.ShapeDtypeStruct((tokens, GROUP * count), jnp.bfloat16),
        scratch_shapes=[
            pltpu.VMEM((ROWS * PARAMS, LANES), jnp.float32),
            pltpu.VMEM((ROWS * ORDER, LANES), jnp.float32),
            pltpu.VMEM((tokens * ROWS, LANES), jnp.float32),
        ],
    )(packed, before, signal, query)


def early_kernel(first_ref, second_ref, far_ref, upper_ref, lower_ref, matrix_ref, done_ref, sum_ref, rows_ref, half_ref):
    tokens, split = first_ref.shape
    rows_ref[:tokens, :split] = first_ref[...]
    rows_ref[:tokens, split:] = second_ref[...]
    rows_ref[tokens:, :] = far_ref[...]
    half_ref[:tokens, :] = upper_ref[...]
    half_ref[tokens:, :] = lower_ref[...]
    for n in range(0, done_ref.shape[1], COLUMNS):
        columns = slice(n, n + COLUMNS)
        product = jnp.dot(rows_ref[...], matrix_ref[:, columns], preferred_element_type=jnp.float32)
        done_ref[:, columns] = product.astype(jnp.bfloat16)
        sum_ref[:, columns] = jnp.dot(
            half_ref[...], matrix_ref[:split, columns], preferred_element_type=jnp.float32
        )


def early_rows(first, second, far, upper, lower, matrix):
    whole = pl.BlockSpec(memory_space=pltpu.VMEM)
    tokens, columns = far.shape[0], matrix.shape[1]
    return call(
        early_kernel,
        "early_rows",
        in_specs=[whole] * 6,
        out_specs=[whole] * 2,
        out_shape=[
            jax.ShapeDtypeStruct((2 * tokens, columns), jnp.bfloat16),
            jax.ShapeDtypeStruct((2 * tokens, columns), jnp.float32),
        ],
        scratch_shapes=[
            pltpu.VMEM((2 * tokens, far.shape[1]), jnp.bfloat16),
            pltpu.VMEM((2 * tokens, first.shape[1]), jnp.bfloat16),
        ],
    )(first, second, far, upper, lower, matrix)


def finish_kernel(place_ref, done_ref, sum_ref, upper_ref, lower_ref, matrix_ref, out_ref, rows_ref):
    tokens, depth = upper_ref.shape
    rows_ref[:tokens, :] = upper_ref[...]
    rows_ref[tokens:, :] = lower_ref[...]
    own, up, far, low = [lax.rem(place_ref[0] + r, 4) for r in range(4)]
    out_ref[own] = done_ref[:tokens, :]
    out_ref[far] = done_ref[tokens:, :]
    for n in range(0, out_ref.shape[2], COLUMNS):
        columns = slice(n, n + COLUMNS)
        matrix = matrix_ref[matrix_ref.shape[0] - depth :, columns]
        product = jnp.dot(rows_ref[...], matrix, preferred_element_type=jnp.float32)
        total = (sum_ref[:, columns] + product).astype(jnp.bfloat16)
        out_ref[up, :, columns] = total[:tokens]
        out_ref[low, :, columns] = total[tokens:]


def finish(z, done, early_sum, upper, lower, matrix):
    tokens, depth = upper.shape
    whole = pl.BlockSpec(memory_space=pltpu.VMEM)
    return call(
        finish_kernel,
        "finish",
        in_specs=[pl.BlockSpec(memory_space=pltpu.SMEM)] + [whole] * 5,
        out_specs=whole,
        out_shape=jax.ShapeDtypeStruct((4, tokens, matrix.shape[1]), jnp.bfloat16),
        scratch_shapes=[pltpu.VMEM((2 * tokens, depth), jnp.bfloat16)],
    )(z.reshape(1), done, early_sum, upper, lower, matrix)


def on_device(query_rows, key_rows, value_rows, residue, pole_rate, skip_gain, out_weight):
    tokens, width = query_rows.shape
    seq_count = lax.axis_size("seq")
    length = tokens * seq_count * lax.axis_size("chan")
    z = lax.axis_index("seq")
    half = width // GROUP // 2

    def from_seq(array, s):
        return lax.ppermute(array, "seq", [(i, (i + s) % seq_count) for i in range(seq_count)])

    def to_owners(array):
        return lax.all_to_all(array, "chan", split_axis=0, concat_axis=0, tiled=True)

    rate = pole_rate / length
    weight = (residue * jnp.sqrt(2.0 * rate)).T
    rate = rate.T
    far_query = from_seq(query_rows, 2)
    signal = make_signal(key_rows, value_rows)
    received = to_owners(signal)
    received, out_weight = lax.optimization_barrier((received, out_weight))
    full_weight = lax.all_gather(out_weight, "chan", axis=0, tiled=True)
    received, far_query = lax.optimization_barrier((received, far_query))

    prefix, total = block_states(tokens, rate, received)
    totals = [from_seq(total, s) for s in (1, 2, 3)]
    totals, signal = lax.optimization_barrier((totals, signal))
    far_signal = from_seq(signal, 2)
    packed = states_before(tokens, z, rate, weight, skip_gain[None, :], prefix, totals)
    packed = to_owners(packed)
    far_before = from_seq(packed[:, PARAMS:], 2)
    first = gate_rows(packed, packed, signal, query_rows, 0, half)
    first, far_before, far_signal = lax.optimization_barrier((first, far_before, far_signal))
    low_first, up_first = from_seq(first, 1), from_seq(first, -1)
    second = gate_rows(packed, packed, signal, query_rows, half, half)
    low_second, up_second = from_seq(second, 1), from_seq(second, -1)
    second, far_before = lax.optimization_barrier((second, far_before))
    far = gate_rows(packed, far_before, far_signal, far_query, 0, 2 * half, 20 * 1024 * 1024)
    done, early_sum = early_rows(first, second, far, up_first, low_first, full_weight)
    return finish(z, done, early_sum, up_second, low_second, full_weight)


def solution(mesh):
    in_specs = (
        P(("seq", "chan"), None),
        P(("seq", "chan"), None),
        P(("seq", "chan"), None),
        P("chan", None),
        P("chan", None),
        P("chan"),
        P("chan", "seq"),
    )
    out_specs = P(None, "chan", "seq")
    return jax.shard_map(
        on_device, mesh=mesh, in_specs=in_specs, out_specs=out_specs, check_vma=False
    )
```

```python
import functools

import jax
import jax.numpy as jnp
from jax import lax
from jax.experimental import pallas as pl
from jax.experimental.pallas import tpu as pltpu
from jax.sharding import PartitionSpec as P

ORDER = 16
LANES = 128
ROWS = 8
GROUP = ROWS * LANES
UNROLL = 8
SLICE = 32
PARAMS = 5 * ORDER
SMALL_LIMIT = 16 * 1024 * 1024
LARGE_LIMIT = 56 * 1024 * 1024
COLUMNS = 512


def call(kernel, name, limit=SMALL_LIMIT, moved=1024, **keywords):
    return pl.pallas_call(
        kernel,
        name=name,
        compiler_params=pltpu.CompilerParams(vmem_limit_bytes=limit),
        cost_estimate=pl.CostEstimate(flops=1024, bytes_accessed=moved, transcendentals=0),
        **keywords,
    )


def as_float(block):
    return block.astype(jnp.float32)


def tree_sum(terms):
    while len(terms) > 1:
        terms = [a + b for a, b in zip(terms[::2], terms[1::2])] + terms[len(terms) & ~1 :]
    return terms[0]


def over_tokens(tokens, step, held):
    def several(outer, held):
        for u in range(UNROLL):
            held = step(pl.multiple_of((outer * UNROLL + u) * ROWS, ROWS), held)
        return held

    return lax.fori_loop(0, tokens // UNROLL, several, held)


def signal_kernel(key_hbm, value_hbm, signal_ref, key_ref, value_ref, sems):
    parts = sems.shape[1]
    size = key_ref.shape[0] // parts
    copies = []
    for n in range(parts):
        rows = pl.ds(n * size, size)
        for at, (source, target) in enumerate([(key_hbm, key_ref), (value_hbm, value_ref)]):
            copies.append(pltpu.make_async_copy(source.at[rows, :], target.at[rows, :], sems.at[at, n]))
            copies[-1].start()
    for n in range(parts):
        copies[2 * n].wait()
        copies[2 * n + 1].wait()
        rows = slice(n * size, (n + 1) * size)
        for j in range(signal_ref.shape[0]):
            columns = slice(j * LANES, (j + 1) * LANES)
            product = as_float(key_ref[rows, columns]) * as_float(value_ref[rows, columns])
            signal_ref[j, rows, :] = product.astype(jnp.bfloat16)


def make_signal(key_rows, value_rows):
    tokens, width = key_rows.shape
    outside = pl.BlockSpec(memory_space=pltpu.HBM)
    return call(
        signal_kernel,
        "signal",
        in_specs=[outside, outside],
        out_specs=pl.BlockSpec(memory_space=pltpu.VMEM),
        out_shape=jax.ShapeDtypeStruct((width // LANES, tokens, LANES), jnp.bfloat16),
        scratch_shapes=[
            pltpu.VMEM((tokens, width), jnp.bfloat16),
            pltpu.VMEM((tokens, width), jnp.bfloat16),
            pltpu.SemaphoreType.DMA((2, tokens // SLICE)),
        ],
    )(key_rows, value_rows)


def states_kernel(tokens, rate_ref, signal_ref, prefix_ref, total_ref, work_ref, state_ref):
    for j in range(ROWS):
        work_ref[pl.ds(j, tokens, stride=ROWS), :] = as_float(signal_ref[j])
    rate = rate_ref[...]
    retain = [
        jnp.broadcast_to(jnp.exp(-rate[m : m + 1, :]), (ROWS, LANES)) for m in range(ORDER)
    ]

    def step(at, held):
        now = work_ref[pl.ds(at, ROWS), :]
        return [retain[m] * held[m] + now for m in range(ORDER)]

    held = over_tokens(tokens, step, [jnp.zeros((ROWS, LANES), jnp.float32)] * ORDER)
    for m in range(ORDER):
        state_ref[pl.ds(m, ROWS, stride=ORDER), :] = held[m]

    @pl.when(pl.program_id(0) == 0)
    def _():
        total_ref[...] = jnp.zeros_like(total_ref)

    decay = jnp.exp(-rate * float(tokens))
    before = total_ref[...]
    for j in range(ROWS):
        prefix_ref[j * ORDER : (j + 1) * ORDER, :] = before
        before = decay * before + state_ref[j * ORDER : (j + 1) * ORDER, :]
    total_ref[...] = before


def block_states(tokens, rate, received):
    blocks, _, lanes = received.shape
    return call(
        functools.partial(states_kernel, tokens),
        "block_states",
        grid=(blocks // ROWS,),
        in_specs=[
            pl.BlockSpec((ORDER, lanes), lambda g: (0, 0)),
            pl.BlockSpec((ROWS, tokens, lanes), lambda g: (g, 0, 0)),
        ],
        out_specs=[
            pl.BlockSpec((ROWS * ORDER, lanes), lambda g: (g, 0)),
            pl.BlockSpec((ORDER, lanes), lambda g: (0, 0)),
        ],
        out_shape=[
            jax.ShapeDtypeStruct((blocks * ORDER, lanes), jnp.float32),
            jax.ShapeDtypeStruct((ORDER, lanes), jnp.float32),
        ],
        scratch_shapes=[
            pltpu.VMEM((tokens * ROWS, lanes), jnp.float32),
            pltpu.VMEM((ROWS * ORDER, lanes), jnp.float32),
        ],
    )(rate, received)


def before_kernel(tokens, place_ref, rate_ref, weight_ref, skip_ref, prefix_ref, *refs):
    *total_refs, packed_ref = refs
    blocks = packed_ref.shape[0]
    rate = rate_ref[...]

    def pair(value):
        high = value.astype(jnp.bfloat16)
        return [high, (value - as_float(high)).astype(jnp.bfloat16)]

    skip = [as_float(part) for part in pair(skip_ref[...])]
    index = lax.broadcasted_iota(jnp.int32, (ORDER, LANES), 0)
    skip = jnp.where(index == 0, skip[0], jnp.where(index == 1, skip[1], 0.0))
    params = pair(rate) + pair(weight_ref[...]) + [skip.astype(jnp.bfloat16)]
    decay = jnp.exp(-rate * float(tokens))
    start = jnp.zeros((ORDER, LANES), jnp.float32)
    for s, total_ref in enumerate(total_refs, 1):
        passed = jnp.exp(-rate * float(tokens * blocks * (s - 1)))
        start = start + jnp.where(place_ref[0] >= s, passed * total_ref[...], 0.0)
    for i in range(blocks):
        for n, part in enumerate(params):
            packed_ref[i, n * ORDER : (n + 1) * ORDER, :] = part
        before = prefix_ref[i * ORDER : (i + 1) * ORDER, :] + start
        packed_ref[i, PARAMS:, :] = before.astype(jnp.bfloat16)
        start = decay * start


def states_before(tokens, z, rate, weight, skip, prefix, totals):
    whole = pl.BlockSpec(memory_space=pltpu.VMEM)
    return call(
        functools.partial(before_kernel, tokens),
        "states_before",
        in_specs=[pl.BlockSpec(memory_space=pltpu.SMEM)] + [whole] * (4 + len(totals)),
        out_specs=whole,
        out_shape=jax.ShapeDtypeStruct(
            (prefix.shape[0] // ORDER, PARAMS + ORDER, LANES), jnp.bfloat16
        ),
    )(z.reshape(1), rate, weight, skip, prefix, *totals)


def gate_kernel(packed_ref, before_ref, signal_ref, query_ref, gated_ref, part_ref, start_ref, work_ref):
    tokens = query_ref.shape[0]
    for j in range(ROWS):
        part_ref[j * PARAMS : (j + 1) * PARAMS, :] = as_float(packed_ref[j])
        start_ref[j * ORDER : (j + 1) * ORDER, :] = as_float(before_ref[j])
        work_ref[pl.ds(j, tokens, stride=ROWS), :] = as_float(signal_ref[j])

    def row(n):
        return part_ref[pl.ds(n, ROWS, stride=PARAMS), :]

    retain = [jnp.exp(-(row(m) + row(ORDER + m))) for m in range(ORDER)]
    weight = [row(2 * ORDER + m) + row(3 * ORDER + m) for m in range(ORDER)]
    skip = row(4 * ORDER) + row(4 * ORDER + 1)
    start = [start_ref[pl.ds(m, ROWS, stride=ORDER), :] for m in range(ORDER)]

    def step(at, held):
        now = work_ref[pl.ds(at, ROWS), :]
        held = [retain[m] * held[m] + now for m in range(ORDER)]
        terms = [weight[m] * held[m] for m in range(ORDER)]
        work_ref[pl.ds(at, ROWS), :] = tree_sum(terms) + skip * now
        return held

    over_tokens(tokens, step, start)
    for j in range(ROWS):
        mixed = work_ref[pl.ds(j, tokens, stride=ROWS), :].astype(jnp.bfloat16)
        columns = slice(j * LANES, (j + 1) * LANES)
        gated = as_float(query_ref[:, columns]) * as_float(mixed)
        gated_ref[:, columns] = gated.astype(jnp.bfloat16)


def gate_rows(packed, before, signal, query, first, count, moved=1024):
    tokens = query.shape[0]
    last = before.shape[1] // ORDER - 1
    return call(
        gate_kernel,
        "gate_rows",
        moved=moved,
        grid=(count,),
        in_specs=[
            pl.BlockSpec((ROWS, PARAMS, LANES), lambda g: (g + first, 0, 0)),
            pl.BlockSpec((ROWS, ORDER, LANES), lambda g: (g + first, last, 0)),
            pl.BlockSpec((ROWS, tokens, LANES), lambda g: (g + first, 0, 0)),
            pl.BlockSpec((tokens, GROUP), lambda g: (0, g + first)),
        ],
        out_specs=pl.BlockSpec((tokens, GROUP), lambda g: (0, g)),
        out_shape=jax.ShapeDtypeStruct((tokens, GROUP * count), jnp.bfloat16),
        scratch_shapes=[
            pltpu.VMEM((ROWS * PARAMS, LANES), jnp.float32),
            pltpu.VMEM((ROWS * ORDER, LANES), jnp.float32),
            pltpu.VMEM((tokens * ROWS, LANES), jnp.float32),
        ],
    )(packed, before, signal, query)


def early_kernel(first_ref, second_ref, far_ref, upper_ref, lower_ref, matrix_ref, late_ref, done_ref, sum_ref, rows_ref, half_ref):
    tokens, split = first_ref.shape
    rows_ref[:tokens, :split] = first_ref[...]
    rows_ref[:tokens, split:] = second_ref[...]
    rows_ref[tokens:, :] = far_ref[...]
    half_ref[:tokens, :] = upper_ref[...]
    half_ref[tokens:, :] = lower_ref[...]
    for n in range(0, done_ref.shape[1], COLUMNS):
        columns = slice(n, n + COLUMNS)
        product = jnp.dot(
            rows_ref[:, :split], matrix_ref[:, columns], preferred_element_type=jnp.float32
        )
        product += jnp.dot(
            rows_ref[:, split:], late_ref[:, columns], preferred_element_type=jnp.float32
        )
        done_ref[:, columns] = product.astype(jnp.bfloat16)
        sum_ref[:, columns] = jnp.dot(
            half_ref[...], late_ref[:, columns], preferred_element_type=jnp.float32
        )


def early_rows(first, second, far, upper, lower, matrix, late):
    whole = pl.BlockSpec(memory_space=pltpu.VMEM)
    tokens, columns = far.shape[0], matrix.shape[1]
    return call(
        early_kernel,
        "early_rows",
        in_specs=[whole] * 7,
        out_specs=[whole] * 2,
        out_shape=[
            jax.ShapeDtypeStruct((2 * tokens, columns), jnp.bfloat16),
            jax.ShapeDtypeStruct((2 * tokens, columns), jnp.float32),
        ],
        scratch_shapes=[
            pltpu.VMEM((2 * tokens, far.shape[1]), jnp.bfloat16),
            pltpu.VMEM((2 * tokens, first.shape[1]), jnp.bfloat16),
        ],
    )(first, second, far, upper, lower, matrix, late)


def finish_kernel(place_ref, done_ref, sum_ref, upper_ref, lower_ref, matrix_ref, out_ref, rows_ref):
    tokens = upper_ref.shape[0]
    rows_ref[:tokens, :] = upper_ref[...]
    rows_ref[tokens:, :] = lower_ref[...]
    own, up, far, low = [lax.rem(place_ref[0] + r, 4) for r in range(4)]
    out_ref[own] = done_ref[:tokens, :]
    out_ref[far] = done_ref[tokens:, :]
    for n in range(0, out_ref.shape[2], COLUMNS):
        columns = slice(n, n + COLUMNS)
        product = jnp.dot(rows_ref[...], matrix_ref[:, columns], preferred_element_type=jnp.float32)
        total = (sum_ref[:, columns] + product).astype(jnp.bfloat16)
        out_ref[up, :, columns] = total[:tokens]
        out_ref[low, :, columns] = total[tokens:]


def finish(z, done, early_sum, upper, lower, matrix):
    tokens, depth = upper.shape
    whole = pl.BlockSpec(memory_space=pltpu.VMEM)
    return call(
        finish_kernel,
        "finish",
        in_specs=[pl.BlockSpec(memory_space=pltpu.SMEM)] + [whole] * 5,
        out_specs=whole,
        out_shape=jax.ShapeDtypeStruct((4, tokens, matrix.shape[1]), jnp.bfloat16),
        scratch_shapes=[pltpu.VMEM((2 * tokens, depth), jnp.bfloat16)],
    )(z.reshape(1), done, early_sum, upper, lower, matrix)


def on_device(query_rows, key_rows, value_rows, residue, pole_rate, skip_gain, out_weight):
    tokens, width = query_rows.shape
    seq_count = lax.axis_size("seq")
    length = tokens * seq_count * lax.axis_size("chan")
    z = lax.axis_index("seq")
    half = width // GROUP // 2

    def from_seq(array, s):
        return lax.ppermute(array, "seq", [(i, (i + s) % seq_count) for i in range(seq_count)])

    def to_owners(array):
        return lax.all_to_all(array, "chan", split_axis=0, concat_axis=0, tiled=True)

    rate = pole_rate / length
    weight = (residue * jnp.sqrt(2.0 * rate)).T
    rate = rate.T
    far_query = from_seq(query_rows, 2)
    signal = make_signal(key_rows, value_rows)
    received = to_owners(signal)
    received, far_query, out_weight = lax.optimization_barrier((received, far_query, out_weight))
    full_weight = lax.all_gather(out_weight, "chan", axis=0, tiled=True)

    prefix, total = block_states(tokens, rate, received)
    totals = [from_seq(total, s) for s in (1, 2, 3)]
    totals, signal = lax.optimization_barrier((totals, signal))
    far_signal = from_seq(signal, 2)
    packed = states_before(tokens, z, rate, weight, skip_gain[None, :], prefix, totals)
    packed = to_owners(packed)
    far_before = from_seq(packed[:, PARAMS:], 2)
    first = gate_rows(packed, packed, signal, query_rows, 0, half)
    first, far_before, far_signal = lax.optimization_barrier((first, far_before, far_signal))
    low_first, up_first = from_seq(first, 1), from_seq(first, -1)
    second = gate_rows(packed, packed, signal, query_rows, half, half)
    low_second, up_second = from_seq(second, 1), from_seq(second, -1)
    second, far_before = lax.optimization_barrier((second, far_before))
    far = gate_rows(packed, far_before, far_signal, far_query, 0, 2 * half, 20 * 1024 * 1024)
    split = half * GROUP
    soon, late = full_weight[:split], full_weight[split:]
    done, early_sum = early_rows(first, second, far, up_second, low_second, soon, late)
    return finish(z, done, early_sum, up_first, low_first, soon)


def solution(mesh):
    in_specs = (
        P(("seq", "chan"), None),
        P(("seq", "chan"), None),
        P(("seq", "chan"), None),
        P("chan", None),
        P("chan", None),
        P("chan"),
        P("chan", "seq"),
    )
    out_specs = P(None, "chan", "seq")
    return jax.shard_map(
        on_device, mesh=mesh, in_specs=in_specs, out_specs=out_specs, check_vma=False
    )
```
